32 devices in a mesh: groups: 2 (over y), view: 4 (over z), gz: 2 (over x), tube: 2 (over core).
Axes of the slice: x: 2, y: 2, z: 4, core: 2. Of those that a mesh axis runs over, the one named last changes fastest.
Arguments:
- fan_views: bfloat16 [4, 2, 128, 64, 1024], P(('groups', 'tube'), 'gz', 'view'), parts along dimension 0, may hold values from -6 to 6
- offsets: int32 [4, 2, 128], P(('groups', 'tube'), 'gz', 'view'), parts along dimension 0, may hold values from 0 to 16
- rebin_matrix: bfloat16 [1024, 1024], replicated, may hold values from -0.1875 to 0.1875
- projector: bfloat16 [2, 16, 512, 256], P('tube'), as said below
- tile_index: int32 [2, 16, 2], P('tube'), may hold values from 0 to 15, as said below
- attenuation: float32 [2, 2], replicated, may hold values from 0.3 to 3
- images: float32 [2, 4, 64, 4096], P(None, ('groups', 'gz'), 'view'), parts along dimension 1, may hold values from 0.5 to 1.5
Outputs:
- sinogram: bfloat16 [4, 2, 64, 128, 1024], P(('groups', 'tube'), 'gz', 'view'), parts along dimension 0
- updated: float32 [2, 4, 64, 4096], P('tube', ('groups', 'gz'), 'view'), parts along dimension 1
The draws below stay inside these ranges and needn't reach their ends.
There are 2 independent parts, one for each index of `groups`. The reference program is written for one: setup_inputs(seed, part) draws one part's arguments, and reference() takes and returns one part's arrays. A program takes and returns all parts, laid end to end along the dimension named above; an argument that names none is the same for every part. Nothing has to cross between parts.
Inputs may be any that keep to these rules, and one draw needn't show every extreme that they name: `projector`: entries are positive. `tile_index`: in each tube's list, column 0 names each of the 16 sinogram blocks once and column 1 names each of the 8 image rows 16 // 8 times.
All inputs are finite; a program needn't handle non-finite values.
Results may differ from the reference program's by a relative error of at most 0.0016.
Values may be sent and summed in bfloat16 or wider, within the bound.
A program may use at most 64 MiB of HBM per device.

```python
import math
import jax
import jax.numpy as jnp
from jax import lax

DC = 1024
DR = 64
IMG = 512
CB = 256
SUB = 4
HZ = 16
IR = 8
SLABS = 2
ANG = 128
K = 16
NPIX = 4096


def draw_projector(key, part):
    key = jax.random.fold_in(key, 17)
    base_key, row_key, col_key = jax.random.split(key, 3)
    base = jax.random.uniform(base_key, (2, K, IMG, CB), jnp.float32, 0.1, 1.0)
    row_scale = jnp.exp(jax.random.uniform(row_key, (2, K, IMG, 1), jnp.float32) * math.log(10.0))
    col_scale = jnp.exp(jax.random.uniform(col_key, (2, K, 1, CB), jnp.float32) * math.log(10.0))
    return (base * row_scale * col_scale / (5.0 * IMG)).astype(jnp.bfloat16)


def draw_tile_index(key, part):
    key = jax.random.fold_in(key, 29)
    keys = jax.random.split(key, 4)
    pattern = jnp.arange(K, dtype=jnp.int32) % IR
    blocks = jnp.stack([jax.random.permutation(keys[0], K), jax.random.permutation(keys[1], K)])
    row_list = jnp.stack([jax.random.permutation(keys[2], pattern), jax.random.permutation(keys[3], pattern)])
    return jnp.stack([blocks.astype(jnp.int32), row_list.astype(jnp.int32)], axis=-1)


def touch_ends(array, stream_key, smallest, largest):
    dims = array.shape
    spot = [jax.random.randint(jax.random.fold_in(stream_key, axis), (), 0, dims[axis]) for axis in range(len(dims))]
    array = array.at[tuple(spot)].set(smallest)
    longest = dims.index(max(dims))
    spot[longest] = (spot[longest] + 1) % dims[longest]
    return array.at[tuple(spot)].set(largest)


def level_of(key, extent, shards, least, high):
    def one(axis_at, shards_of):
        steps = jax.random.uniform(jax.random.fold_in(jax.random.fold_in(key, 6), axis_at), (shards_of,), jnp.float32, least / len(shards), high / len(shards))
        return jnp.repeat(jnp.exp(steps), extent[axis_at] // shards_of).reshape((-1,) + (1,) * (len(extent) - axis_at - 1))

    loudness = one(*shards[0])
    for cut in shards[1:]:
        loudness = loudness * one(*cut)
    return loudness


def gaussian(stream_key, extent, scale, bound, cuts=(), held_as=jnp.bfloat16):
    loudness = level_of(stream_key, extent, cuts, -0.22, 0.18) if cuts else 1.0
    drawn = jax.random.normal(stream_key, extent, jnp.float32) * scale * loudness
    return jnp.minimum(jnp.maximum(drawn, -bound), bound).astype(held_as)


def setup_inputs(seed: int = 0, part: int = 0) -> dict:
    splits = jax.random.split(jax.random.key(seed), 8)
    part_keys = jax.random.split(jax.random.fold_in(splits[7], part), 8)
    return {
        "fan_views": gaussian(part_keys[0], (2, SLABS, ANG, DR, DC), 1.0, 6.0, ((0, 2), (1, 2), (2, 4))),
        "offsets": touch_ends(jax.random.randint(part_keys[1], (2, SLABS, ANG), 0, HZ + 1), jax.random.fold_in(part_keys[1], 1), 0, HZ).astype(jnp.int32),
        "rebin_matrix": gaussian(splits[2], (DC, DC), DC ** -0.5, 0.1875),
        "projector": draw_projector(jax.random.fold_in(splits[7], 71), part),
        "tile_index": draw_tile_index(jax.random.fold_in(splits[7], 71), part),
        "attenuation": jnp.clip(jnp.exp(jax.random.uniform(splits[5], (2, 2), jnp.float32, math.log(0.3), math.log(3.0))), 0.3, 3.0),
        "images": jnp.clip(0.5 + 1.0 * jax.random.uniform(part_keys[6], (2, SLABS, DR, NPIX), jnp.float32) ** level_of(part_keys[6], (2, SLABS, DR, NPIX), ((1, 2), (2, 4)), -0.2, 0.2), 0.5, 1.5),
    }


relax_factor = 0.8


def round_bf16(values):
    return lax.optimization_barrier(values.astype(jnp.bfloat16)).astype(jnp.float32)


def place_views(fan_slab, lower_rim, offset_list):
    extended = jnp.concatenate([lower_rim, fan_slab], axis=1)

    def pick_rows(view_rows, offset):
        return lax.dynamic_slice_in_dim(view_rows, (HZ - offset).astype(jnp.int32), DR, 0)

    return jax.vmap(pick_rows)(extended, offset_list)


def reference(fan_views, offsets, rebin_matrix, projector, tile_index, attenuation, images):
    sinograms = []
    for tube_number in range(2):
        slab_list = []
        for slab_index in range(SLABS):
            if slab_index > 0:
                lower_rim = fan_views[tube_number, slab_index - 1, :, DR - HZ:, :]
            else:
                lower_rim = jnp.zeros((ANG, HZ, DC), fan_views.dtype)
            placed = place_views(fan_views[tube_number, slab_index], lower_rim, offsets[tube_number, slab_index])
            rebinned = jnp.dot(placed.reshape(-1, DC), rebin_matrix, preferred_element_type=jnp.float32)
            slab_list.append(rebinned.astype(jnp.bfloat16).reshape(ANG, DR, DC).transpose(1, 0, 2))
        sinograms.append(jnp.stack(slab_list))
    sinogram = jnp.stack(sinograms)
    total_rows = SLABS * DR
    numerator = jnp.zeros((2, total_rows, NPIX), jnp.float32)
    denominator = jnp.zeros((2, NPIX), jnp.float32)
    for tube_number in range(2):
        measured = sinogram[tube_number][:, :, ::(ANG // SUB), :].reshape(total_rows, K, CB).astype(jnp.float32)
        weights = attenuation[tube_number]
        combined = round_bf16(weights[0] * images[0] + weights[1] * images[1]).reshape(total_rows, IR, IMG)
        tile_data = projector[tube_number].astype(jnp.float32)
        blocks = tile_index[tube_number, :, 0]
        row_list = tile_index[tube_number, :, 1]
        chosen = jnp.take(combined, row_list, axis=1)
        projected_tiles = jnp.einsum("rkp,kpc->rkc", chosen, tile_data, precision=lax.Precision.HIGHEST)
        projected = jnp.zeros((total_rows, K, CB), jnp.float32).at[:, blocks].add(projected_tiles)
        ray_sum = jnp.zeros((K, CB), jnp.float32).at[blocks].add(jnp.sum(tile_data, axis=1))
        residual = round_bf16((measured - projected) / ray_sum)
        tile_residual = jnp.take(residual, blocks, axis=1)
        back_tiles = jnp.einsum("rkc,kpc->rkp", tile_residual, tile_data, precision=lax.Precision.HIGHEST)
        back_projection = jnp.zeros((total_rows, IR, IMG), jnp.float32).at[:, row_list].add(back_tiles)
        back_projection = back_projection.reshape(total_rows, NPIX)
        pixel_sum = jnp.zeros((IR, IMG), jnp.float32).at[row_list].add(jnp.sum(tile_data, axis=2)).reshape(NPIX)
        numerator = numerator + weights[:, None, None] * back_projection[None]
        denominator = denominator + weights[:, None] * pixel_sum[None]
    updated = images.reshape(2, total_rows, NPIX) + relax_factor * (numerator / denominator[:, None, :])
    return sinogram, updated.reshape(2, SLABS, DR, NPIX)
```

```python
import functools

import jax
import jax.numpy as jnp
from jax import lax
from jax.experimental import pallas as pl
from jax.experimental.pallas import tpu as pltpu
from jax.sharding import PartitionSpec as P

IMG = 512
CB = 256
SUB = 4
HZ = 16
IR = 8
BLK = 16
MESH = pl.DeviceIdType.MESH

relax_factor = 0.8


def kernel(
    sizes,
    offsets_ref,
    index_ref,
    weight_ref,
    fan_ref,
    rebin_ref,
    projector_ref,
    images_ref,
    sino_ref,
    updated_ref,
    ext,
    rebin,
    tiles,
    material,
    stage,
    comb,
    proj,
    picked,
    meas,
    back,
    give,
    keep,
    take,
    own_sem,
    rebin_sem,
    tiles_sem,
    image_sem,
    top_send,
    top_recv,
    out_send,
    out_recv,
    self_sem,
    picked_sem,
    tube_send,
    tube_recv,
):
    views, slabs, angles, rows, slices = sizes
    groups = angles // BLK
    blocks = rows // BLK
    share = BLK // slices
    tile_count = tiles.shape[0]
    per_angle = tile_count // SUB
    stride = views * angles // SUB
    me = lax.axis_index("view")
    slab = lax.axis_index("gz")
    tube = lax.axis_index("tube")

    def own_copy(g):
        return pltpu.make_async_copy(
            fan_ref.at[pl.ds(g * BLK, BLK)],
            ext.at[pl.ds(g * BLK, BLK), pl.ds(HZ, rows), :],
            own_sem.at[g],
        )

    rebin_copy = pltpu.make_async_copy(rebin_ref, rebin, rebin_sem)
    tiles_copy = pltpu.make_async_copy(projector_ref, tiles, tiles_sem)
    image_copy = pltpu.make_async_copy(images_ref, material, image_sem)
    own_copy(0).start()
    rebin_copy.start()
    for g in range(1, groups):
        own_copy(g).start()
    image_copy.start()
    tiles_copy.start()

    barrier = pltpu.get_barrier_semaphore()

    def greet(v, carry):
        @pl.when(v != me)
        def _():
            pl.semaphore_signal(barrier, inc=1, device_id={"view": v}, device_id_type=MESH)

        return carry

    lax.fori_loop(0, views, greet, 0)
    pl.semaphore_signal(barrier, inc=1, device_id={"tube": 1 - tube}, device_id_type=MESH)

    @pl.when(slab > 0)
    def _():
        pl.semaphore_signal(barrier, inc=1, device_id={"gz": slab - 1}, device_id_type=MESH)

    @pl.when(slab < slabs - 1)
    def _():
        pl.semaphore_signal(barrier, inc=1, device_id={"gz": slab + 1}, device_id_type=MESH)

    edges = jnp.where(slab > 0, 1, 0) + jnp.where(slab < slabs - 1, 1, 0)
    pl.semaphore_wait(barrier, views + edges)

    def top_copy(g):
        return pltpu.make_async_remote_copy(
            src_ref=fan_ref.at[pl.ds(g * BLK, BLK), pl.ds(rows - HZ, HZ), :],
            dst_ref=ext.at[pl.ds(g * BLK, BLK), pl.ds(0, HZ), :],
            send_sem=top_send.at[g],
            recv_sem=top_recv.at[g],
            device_id={"gz": jnp.minimum(slab + 1, slabs - 1)},
            device_id_type=MESH,
        )

    @pl.when(slab < slabs - 1)
    def _():
        for g in range(groups):
            top_copy(g).start()

    @pl.when(slab == 0)
    def _():
        ext[:, 0:HZ, :] = jnp.zeros((angles, HZ, ext.shape[2]), ext.dtype)

    def out_copy(g, b, j):
        return pltpu.make_async_remote_copy(
            src_ref=stage.at[g, b, pl.ds(j * slices, slices)],
            dst_ref=sino_ref.at[:, pl.ds(pl.multiple_of(me * angles + g * BLK, BLK), BLK), :],
            send_sem=out_send.at[g, b, j],
            recv_sem=out_recv.at[g, me],
            device_id={"view": b * share + j},
            device_id_type=MESH,
        )

    def self_copy(g, b, j):
        return pltpu.make_async_copy(
            stage.at[g, b, pl.ds(j * slices, slices)],
            sino_ref.at[:, pl.ds(pl.multiple_of(me * angles + g * BLK, BLK), BLK), :],
            self_sem.at[g],
        )

    def send(g, b):
        for j in range(share):
            there = b * share + j

            @pl.when(there != me)
            def _():
                out_copy(g, b, j).start()

            @pl.when(there == me)
            def _():
                self_copy(g, b, j).start()

    def sent(g, b):
        for j in range(share):

            @pl.when(b * share + j != me)
            def _():
                out_copy(g, b, j).wait_send()

    def arrived(g, v):
        @pl.when(v != me)
        def _():
            pltpu.make_async_remote_copy(
                src_ref=stage.at[g, 0, pl.ds(0, slices)],
                dst_ref=sino_ref.at[:, pl.ds(v * angles + g * BLK, BLK), :],
                send_sem=out_send.at[g, 0, 0],
                recv_sem=out_recv.at[g, v],
                device_id={"view": v},
                device_id_type=MESH,
            ).wait_recv()

        @pl.when(v == me)
        def _():
            self_copy(g, 0, 0).wait()

    half = blocks // 2
    low = me * slices // BLK < half

    def block_of(i):
        up = jnp.where(i < half, i + half, i - half + 1)
        b = jnp.where(low, up, i + 1)
        return jnp.where(i == blocks - 1, 0, b)

    def work(g):
        own_copy(g).wait()
        shape = (BLK * BLK, BLK * 2 * BLK)
        row = lax.broadcasted_iota(jnp.int32, shape, 0)
        column = lax.broadcasted_iota(jnp.int32, shape, 1)
        lane_angle = lax.broadcasted_iota(jnp.int32, (8, shape[1]), 1) >> 5
        moved = jnp.zeros((8, shape[1]), jnp.int32)
        for a in range(BLK):
            moved = jnp.where(lane_angle == a, offsets_ref[g * BLK + a], moved)
        hit = ((row & 15) == (column >> 5)) & ((row >> 4) + HZ - (column & 31) == moved[0:1])
        chosen = jnp.where(hit, 1.0, 0.0).astype(jnp.bfloat16)

        def unit(i, carry):
            b = block_of(i)

            @pl.when((i == blocks - 1) & (slab > 0))
            def _():
                top_copy(g).wait_recv()

            window = ext[pl.ds(g * BLK, BLK), pl.ds(pl.multiple_of(b * BLK, BLK), 2 * BLK), :]
            window = window.reshape(BLK * 2 * BLK, window.shape[2])
            placed = jnp.dot(chosen, window, preferred_element_type=jnp.float32)
            rebinned = jnp.dot(
                placed.astype(jnp.bfloat16), rebin[...], preferred_element_type=jnp.float32
            )
            rebinned = rebinned.astype(jnp.bfloat16)
            stage[g, b] = rebinned.reshape(BLK, BLK, rebinned.shape[1])
            if g == 0:
                send(g, b)
            return carry

        lax.fori_loop(0, blocks, unit, 0)

    rebin_copy.wait()
    for g in range(groups):
        work(g)

    image_copy.wait()
    w0 = weight_ref[tube, 0]
    w1 = weight_ref[tube, 1]
    for r in range(IR):
        part = slice(r * IMG, (r + 1) * IMG)
        mixed = (w0 * material[0, :, part] + w1 * material[1, :, part]).astype(jnp.bfloat16)
        comb[r, 0:BLK] = mixed
        comb[r, BLK : 2 * BLK] = jnp.ones((BLK, IMG), jnp.bfloat16)
    tiles_copy.wait()

    def forward(k, carry):
        proj[k] = jnp.dot(comb[index_ref[k, 1]], tiles[k], preferred_element_type=jnp.float32)
        return carry

    lax.fori_loop(0, tile_count, forward, 0)

    for g in range(1, groups):

        def follow(i, carry):
            b = block_of(i)
            sent(g - 1, b)
            send(g, b)
            return carry

        lax.fori_loop(0, blocks, follow, 0)

    early = []
    for q in range(SUB):
        v, local = divmod(q * stride, angles)
        if (local // BLK, v) not in early:
            early.append((local // BLK, v))
            arrived(local // BLK, v)
    fetches = [
        pltpu.make_async_copy(
            sino_ref.at[:, pl.ds(q * stride // BLK * BLK, BLK), :],
            picked.at[q],
            picked_sem.at[q],
        )
        for q in range(SUB)
    ]
    for fetch in fetches:
        fetch.start()
    for q in range(SUB):
        fetches[q].wait()
        shape = (BLK, slices * BLK)
        row = lax.broadcasted_iota(jnp.int32, shape, 0)
        column = lax.broadcasted_iota(jnp.int32, shape, 1)
        pick = jnp.where(row * BLK + q * stride % BLK == column, 1.0, 0.0).astype(jnp.bfloat16)
        near = picked[q].reshape(slices * BLK, picked.shape[3])
        line = jnp.dot(pick, near, preferred_element_type=jnp.float32)
        for c in range(per_angle):
            meas[q * per_angle + c] = line[:, c * CB : (c + 1) * CB]

    def backward(k, carry):
        projected = proj[k]
        residual = (meas[index_ref[k, 0]] - projected[0:BLK]) / projected[BLK : BLK + 1]
        left = jnp.concatenate([residual, jnp.ones_like(residual)], axis=0).astype(jnp.bfloat16)
        back[k] = lax.dot_general(
            left, tiles[k], (((1,), (1,)), ((), ())), preferred_element_type=jnp.float32
        )
        return carry

    lax.fori_loop(0, tile_count, backward, 0)

    held = give.shape[1]
    for r in range(IR):

        def gather(k, total):
            same = jnp.full((held, IMG), index_ref[k, 1], jnp.int32) == r
            return total + jnp.where(same, back[k, 0:held], 0.0)

        total_of_row = lax.fori_loop(0, tile_count, gather, jnp.zeros((held, IMG), jnp.float32))
        give[r] = weight_ref[tube, 1 - tube] * total_of_row
        keep[r] = weight_ref[tube, tube] * total_of_row
    tube_copy = pltpu.make_async_remote_copy(
        src_ref=give,
        dst_ref=take,
        send_sem=tube_send,
        recv_sem=tube_recv,
        device_id={"tube": 1 - tube},
        device_id_type=MESH,
    )
    tube_copy.start()
    tube_copy.wait()
    for r in range(IR):
        part = slice(r * IMG, (r + 1) * IMG)
        both = keep[r] + take[r]
        updated_ref[:, part] = material[tube, :, part] + relax_factor * (
            both[0:BLK] / both[BLK : BLK + 1]
        )

    def last(i, carry):
        sent(groups - 1, i)
        return carry

    lax.fori_loop(0, blocks, last, 0)
    for g in range(groups):
        for v in range(views):
            if (g, v) not in early:
                arrived(g, v)

    @pl.when(slab < slabs - 1)
    def _():
        for g in range(groups):
            top_copy(g).wait_send()


def body(views, slabs, fan_views, offsets, rebin_matrix, projector, tile_index, attenuation, images):
    angles, rows, channels = fan_views.shape[2:]
    slices = images.shape[2]
    groups = angles // BLK
    blocks = rows // BLK
    share = BLK // slices
    tile_count = projector.shape[1]
    pixels = images.shape[3]
    material = images[:, 0]
    if slices < BLK:
        material = jnp.pad(material, ((0, 0), (0, BLK - slices), (0, 0)))
    held = BLK + 8
    bf16, f32 = jnp.bfloat16, jnp.float32
    dma = pltpu.SemaphoreType.DMA
    vmem = pltpu.VMEM
    smem = pl.BlockSpec(memory_space=pltpu.SMEM)
    anywhere = pl.BlockSpec(memory_space=pl.ANY)
    sinogram, updated = pl.pallas_call(
        functools.partial(kernel, (views, slabs, angles, rows, slices)),
        out_shape=(
            jax.ShapeDtypeStruct((slices, views * angles, channels), bf16),
            jax.ShapeDtypeStruct((BLK, pixels), f32),
        ),
        in_specs=[smem, smem, smem, anywhere, anywhere, anywhere, anywhere],
        out_specs=(anywhere, pl.BlockSpec(memory_space=vmem)),
        scratch_shapes=[
            vmem((angles, HZ + rows, channels), bf16),
            vmem((channels, channels), bf16),
            vmem((tile_count, IMG, CB), bf16),
            vmem((2, BLK, pixels), f32),
            vmem((groups, blocks, BLK, BLK, channels), bf16),
            vmem((IR, 2 * BLK, IMG), bf16),
            vmem((tile_count, 2 * BLK, CB), f32),
            vmem((SUB, slices, BLK, channels), bf16),
            vmem((tile_count, BLK, CB), f32),
            vmem((tile_count, 2 * BLK, IMG), f32),
            vmem((IR, held, IMG), f32),
            vmem((IR, held, IMG), f32),
            vmem((IR, held, IMG), f32),
            dma((groups,)),
            dma,
            dma,
            dma,
            dma((groups,)),
            dma((groups,)),
            dma((groups, blocks, share)),
            dma((groups, views)),
            dma((groups,)),
            dma((SUB,)),
            dma,
            dma,
        ],
        compiler_params=pltpu.CompilerParams(
            collective_id=0, has_side_effects=True, vmem_limit_bytes=48 * 1024 * 1024
        ),
        name="rebin_update",
    )(offsets[0, 0], tile_index[0], attenuation, fan_views[0, 0], rebin_matrix, projector[0], material)
    return (sinogram[None, None], updated[None, None, :slices])


def solution(mesh):
    in_specs = (
        P(("groups", "tube"), "gz", "view", None, None),
        P(("groups", "tube"), "gz", "view"),
        P(),
        P("tube", None, None, None),
        P("tube", None, None),
        P(),
        P(None, ("groups", "gz"), "view", None),
    )
    out_specs = (
        P(("groups", "tube"), "gz", "view", None, None),
        P("tube", ("groups", "gz"), "view", None),
    )
    return jax.shard_map(
        functools.partial(body, mesh.shape["view"], mesh.shape["gz"]),
        mesh=mesh,
        in_specs=in_specs,
        out_specs=out_specs,
        check_vma=False,
    )
```

```python
import functools

import jax
import jax.numpy as jnp
from jax import lax
from jax.experimental import pallas as pl
from jax.experimental.pallas import tpu as pltpu
from jax.sharding import PartitionSpec as P

IMG = 512
CB = 256
SUB = 4
HZ = 16
IR = 8
BLK = 16
MESH = pl.DeviceIdType.MESH

relax_factor = 0.8


def kernel(
    sizes,
    offsets_in,
    index_in,
    weight_in,
    fan_ref,
    rebin_ref,
    projector_ref,
    images_ref,
    sino_ref,
    updated_ref,
    offsets_ref,
    index_ref,
    weight_ref,
    ext,
    rebin,
    tiles,
    material,
    stage,
    comb,
    proj,
    picked,
    meas,
    back,
    give,
    keep,
    take,
    own_sem,
    rebin_sem,
    tiles_sem,
    image_sem,
    top_send,
    top_recv,
    out_send,
    out_recv,
    self_sem,
    picked_sem,
    tube_send,
    tube_recv,
    small_sem,
):
    views, slabs, angles, rows, slices = sizes
    groups = angles // BLK
    blocks = rows // BLK
    share = BLK // slices
    tile_count = tiles.shape[0]
    per_angle = tile_count // SUB
    stride = views * angles // SUB
    me = lax.axis_index("view")
    slab = lax.axis_index("gz")
    tube = lax.axis_index("tube")

    half = blocks // 2
    low = me * slices // BLK < half

    def block_of(i):
        up = jnp.where(i < half, i + half, i - half + 1)
        b = jnp.where(low, up, i + 1)
        return jnp.where(i == blocks - 1, 0, b)

    def own_copy(g, p):
        chunk = lax.rem(p + jnp.where(low, half - 1, 0), blocks)
        first = pl.multiple_of(chunk * BLK, BLK)
        return pltpu.make_async_copy(
            fan_ref.at[pl.ds(g * BLK, BLK), pl.ds(first, BLK), :],
            ext.at[pl.ds(g * BLK, BLK), pl.ds(first + HZ, BLK), :],
            own_sem.at[g, p],
        )

    rebin_copy = pltpu.make_async_copy(rebin_ref, rebin, rebin_sem)
    tiles_copy = pltpu.make_async_copy(projector_ref, tiles, tiles_sem)
    image_copy = pltpu.make_async_copy(images_ref, material, image_sem)
    small = [
        pltpu.make_async_copy(offsets_in, offsets_ref, small_sem.at[0]),
        pltpu.make_async_copy(index_in, index_ref, small_sem.at[1]),
        pltpu.make_async_copy(weight_in, weight_ref, small_sem.at[2]),
    ]
    for copy in small:
        copy.start()
    own_copy(0, 0).start()
    own_copy(0, 1).start()
    rebin_copy.start()

    barrier = pltpu.get_barrier_semaphore()

    def greet(v, carry):
        @pl.when(v != me)
        def _():
            pl.semaphore_signal(barrier, inc=1, device_id={"view": v}, device_id_type=MESH)

        return carry

    lax.fori_loop(0, views, greet, 0)
    pl.semaphore_signal(barrier, inc=1, device_id={"tube": 1 - tube}, device_id_type=MESH)

    @pl.when(slab > 0)
    def _():
        pl.semaphore_signal(barrier, inc=1, device_id={"gz": slab - 1}, device_id_type=MESH)

    @pl.when(slab < slabs - 1)
    def _():
        pl.semaphore_signal(barrier, inc=1, device_id={"gz": slab + 1}, device_id_type=MESH)

    edges = jnp.where(slab > 0, 1, 0) + jnp.where(slab < slabs - 1, 1, 0)

    def top_copy(g):
        return pltpu.make_async_remote_copy(
            src_ref=fan_ref.at[pl.ds(g * BLK, BLK), pl.ds(rows - HZ, HZ), :],
            dst_ref=ext.at[pl.ds(g * BLK, BLK), pl.ds(0, HZ), :],
            send_sem=top_send.at[g],
            recv_sem=top_recv.at[g],
            device_id={"gz": jnp.minimum(slab + 1, slabs - 1)},
            device_id_type=MESH,
        )

    @pl.when(slab == 0)
    def _():
        ext[:, 0:HZ, :] = jnp.zeros((angles, HZ, ext.shape[2]), ext.dtype)

    def out_copy(g, b, j):
        return pltpu.make_async_remote_copy(
            src_ref=stage.at[g, b, pl.ds(j * slices, slices)],
            dst_ref=sino_ref.at[:, pl.ds(pl.multiple_of(me * angles + g * BLK, BLK), BLK), :],
            send_sem=out_send.at[g, b, j],
            recv_sem=out_recv.at[g, me],
            device_id={"view": b * share + j},
            device_id_type=MESH,
        )

    def self_copy(g, b, j):
        return pltpu.make_async_copy(
            stage.at[g, b, pl.ds(j * slices, slices)],
            sino_ref.at[:, pl.ds(pl.multiple_of(me * angles + g * BLK, BLK), BLK), :],
            self_sem.at[g],
        )

    def send(g, b):
        for j in range(share):
            there = b * share + j

            @pl.when(there != me)
            def _():
                out_copy(g, b, j).start()

            @pl.when(there == me)
            def _():
                self_copy(g, b, j).start()

    def sent(g, b):
        for j in range(share):

            @pl.when(b * share + j != me)
            def _():
                out_copy(g, b, j).wait_send()

    def arrived(g, v):
        @pl.when(v != me)
        def _():
            pltpu.make_async_remote_copy(
                src_ref=stage.at[g, 0, pl.ds(0, slices)],
                dst_ref=sino_ref.at[:, pl.ds(v * angles + g * BLK, BLK), :],
                send_sem=out_send.at[g, 0, 0],
                recv_sem=out_recv.at[g, v],
                device_id={"view": v},
                device_id_type=MESH,
            ).wait_recv()

        @pl.when(v == me)
        def _():
            self_copy(g, 0, 0).wait()

    def work(g):
        shape = (BLK * BLK, BLK * 2 * BLK)
        row = lax.broadcasted_iota(jnp.int32, shape, 0)
        column = lax.broadcasted_iota(jnp.int32, shape, 1)
        lane_angle = lax.broadcasted_iota(jnp.int32, (8, shape[1]), 1) >> 5
        moved = jnp.zeros((8, shape[1]), jnp.int32)
        for a in range(BLK):
            moved = jnp.where(lane_angle == a, offsets_ref[0, g * BLK + a], moved)
        hit = ((row & 15) == (column >> 5)) & ((row >> 4) + HZ - (column & 31) == moved[0:1])
        chosen = jnp.where(hit, 1.0, 0.0).astype(jnp.bfloat16)

        def unit(i):
            b = block_of(i)
            window = ext[pl.ds(g * BLK, BLK), pl.ds(pl.multiple_of(b * BLK, BLK), 2 * BLK), :]
            window = window.reshape(BLK * 2 * BLK, window.shape[2])
            placed = jnp.dot(chosen, window, preferred_element_type=jnp.float32)
            rebinned = jnp.dot(
                placed.astype(jnp.bfloat16), rebin[...], preferred_element_type=jnp.float32
            )
            rebinned = rebinned.astype(jnp.bfloat16)
            stage[g, b] = rebinned.reshape(BLK, BLK, rebinned.shape[1])

        own_copy(g, 0).wait()
        own_copy(g, 1).wait()
        if g == 0:
            rebin_copy.wait()
            later()
        unit(0)
        if g == 0:
            pl.semaphore_wait(barrier, views + edges)

            @pl.when(slab < slabs - 1)
            def _():
                for h in range(groups):
                    top_copy(h).start()

        send(g, block_of(0))

        def step(i, carry):
            @pl.when(i < blocks - 1)
            def _():
                own_copy(g, i + 1).wait()

            @pl.when((i == blocks - 1) & (slab > 0))
            def _():
                top_copy(g).wait_recv()

            unit(i)
            send(g, block_of(i))
            return carry

        lax.fori_loop(1, blocks, step, 0)

    def later():
        for p in range(2, blocks):
            own_copy(0, p).start()
        for g in range(1, groups):
            for p in range(blocks):
                own_copy(g, p).start()
        image_copy.start()
        tiles_copy.start()

    for copy in small:
        copy.wait()
    for g in range(groups):
        work(g)

    image_copy.wait()
    w0 = weight_ref[tube, 0]
    w1 = weight_ref[tube, 1]
    for r in range(IR):
        part = slice(r * IMG, (r + 1) * IMG)
        mixed = (w0 * material[0, :, part] + w1 * material[1, :, part]).astype(jnp.bfloat16)
        comb[r, 0:BLK] = mixed
        comb[r, BLK : 2 * BLK] = jnp.ones((BLK, IMG), jnp.bfloat16)
    tiles_copy.wait()

    def forward(k, carry):
        proj[k] = jnp.dot(comb[index_ref[1, k]], tiles[k], preferred_element_type=jnp.float32)
        return carry

    lax.fori_loop(0, tile_count, forward, 0)

    early = []
    for q in range(SUB):
        v, local = divmod(q * stride, angles)
        if (local // BLK, v) not in early:
            early.append((local // BLK, v))
            arrived(local // BLK, v)
    fetches = [
        pltpu.make_async_copy(
            sino_ref.at[:, pl.ds(q * stride // BLK * BLK, BLK), :],
            picked.at[q],
            picked_sem.at[q],
        )
        for q in range(SUB)
    ]
    for fetch in fetches:
        fetch.start()
    for q in range(SUB):
        fetches[q].wait()
        shape = (BLK, slices * BLK)
        row = lax.broadcasted_iota(jnp.int32, shape, 0)
        column = lax.broadcasted_iota(jnp.int32, shape, 1)
        pick = jnp.where(row * BLK + q * stride % BLK == column, 1.0, 0.0).astype(jnp.bfloat16)
        near = picked[q].reshape(slices * BLK, picked.shape[3])
        line = jnp.dot(pick, near, preferred_element_type=jnp.float32)
        for c in range(per_angle):
            meas[q * per_angle + c] = line[:, c * CB : (c + 1) * CB]

    def backward(k, carry):
        projected = proj[k]
        residual = (meas[index_ref[0, k]] - projected[0:BLK]) / projected[BLK : BLK + 1]
        left = jnp.concatenate([residual, jnp.ones_like(residual)], axis=0).astype(jnp.bfloat16)
        back[k] = lax.dot_general(
            left, tiles[k], (((1,), (1,)), ((), ())), preferred_element_type=jnp.float32
        )
        return carry

    lax.fori_loop(0, tile_count, backward, 0)

    held = give.shape[1]
    for r in range(IR):

        def gather(k, total):
            same = jnp.full((held, IMG), index_ref[1, k], jnp.int32) == r
            return total + jnp.where(same, back[k, 0:held], 0.0)

        total_of_row = lax.fori_loop(0, tile_count, gather, jnp.zeros((held, IMG), jnp.float32))
        give[r] = weight_ref[tube, 1 - tube] * total_of_row
        keep[r] = weight_ref[tube, tube] * total_of_row
    tube_copy = pltpu.make_async_remote_copy(
        src_ref=give,
        dst_ref=take,
        send_sem=tube_send,
        recv_sem=tube_recv,
        device_id={"tube": 1 - tube},
        device_id_type=MESH,
    )
    tube_copy.start()
    tube_copy.wait()
    for r in range(IR):
        part = slice(r * IMG, (r + 1) * IMG)
        both = keep[r] + take[r]
        updated_ref[:, part] = material[tube, :, part] + relax_factor * (
            both[0:BLK] / both[BLK : BLK + 1]
        )

    def last(i, carry):
        for g in range(groups):
            sent(g, i)
        return carry

    lax.fori_loop(0, blocks, last, 0)
    for g in range(groups):
        for v in range(views):
            if (g, v) not in early:
                arrived(g, v)

    @pl.when(slab < slabs - 1)
    def _():
        for g in range(groups):
            top_copy(g).wait_send()


def body(views, slabs, fan_views, offsets, rebin_matrix, projector, tile_index, attenuation, images):
    angles, rows, channels = fan_views.shape[2:]
    slices = images.shape[2]
    groups = angles // BLK
    blocks = rows // BLK
    share = BLK // slices
    tile_count = projector.shape[1]
    pixels = images.shape[3]
    material = images[:, 0]
    if slices < BLK:
        material = jnp.pad(material, ((0, 0), (0, BLK - slices), (0, 0)))
    held = BLK + 8
    bf16, f32 = jnp.bfloat16, jnp.float32
    dma = pltpu.SemaphoreType.DMA
    vmem = pltpu.VMEM
    inside = slices * views * angles * channels * 2 <= 8 * 1024 * 1024
    landing = vmem if inside else jax.ShapeDtypeStruct
    where = pl.BlockSpec(memory_space=vmem if inside else pl.ANY)
    hbm = pl.BlockSpec(memory_space=pltpu.HBM)
    sinogram, updated = pl.pallas_call(
        functools.partial(kernel, (views, slabs, angles, rows, slices)),
        out_shape=(
            landing((slices, views * angles, channels), bf16),
            vmem((BLK, pixels), f32),
        ),
        in_specs=[hbm] * 7,
        out_specs=(where, pl.BlockSpec(memory_space=vmem)),
        scratch_shapes=[
            pltpu.SMEM((1, angles), jnp.int32),
            pltpu.SMEM((2, tile_count), jnp.int32),
            pltpu.SMEM((2, 2), f32),
            vmem((angles, HZ + rows, channels), bf16),
            vmem((channels, channels), bf16),
            vmem((tile_count, IMG, CB), bf16),
            vmem((2, BLK, pixels), f32),
            vmem((groups, blocks, BLK, BLK, channels), bf16),
            vmem((IR, 2 * BLK, IMG), bf16),
            vmem((tile_count, 2 * BLK, CB), f32),
            vmem((SUB, slices, BLK, channels), bf16),
            vmem((tile_count, BLK, CB), f32),
            vmem((tile_count, 2 * BLK, IMG), f32),
            vmem((IR, held, IMG), f32),
            vmem((IR, held, IMG), f32),
            vmem((IR, held, IMG), f32),
            dma((groups, blocks)),
            dma,
            dma,
            dma,
            dma((groups,)),
            dma((groups,)),
            dma((groups, blocks, share)),
            dma((groups, views)),
            dma((groups,)),
            dma((SUB,)),
            dma,
            dma,
            dma((3,)),
        ],
        compiler_params=pltpu.CompilerParams(
            collective_id=0, has_side_effects=True, vmem_limit_bytes=119 * 512 * 1024
        ),
        name="rebin_update",
    )(offsets[0], tile_index[0].T, attenuation, fan_views[0, 0], rebin_matrix, projector[0], material)
    return (sinogram[None, None], updated[None, None, :slices])


def solution(mesh):
    in_specs = (
        P(("groups", "tube"), "gz", "view", None, None),
        P(("groups", "tube"), "gz", "view"),
        P(),
        P("tube", None, None, None),
        P("tube", None, None),
        P(),
        P(None, ("groups", "gz"), "view", None),
    )
    out_specs = (
        P(("groups", "tube"), "gz", "view", None, None),
        P("tube", ("groups", "gz"), "view", None),
    )
    return jax.shard_map(
        functools.partial(body, mesh.shape["view"], mesh.shape["gz"]),
        mesh=mesh,
        in_specs=in_specs,
        out_specs=out_specs,
        check_vma=False,
    )
```
